128 devices in a mesh: gx: 16 (over x, z), gy: 8 (over y, core).
Axes of the slice: x: 4, y: 4, z: 4, core: 2. Of those that a mesh axis runs over, the one named last changes fastest.
Arguments:
- object_field: bfloat16 [2, 2, 4096, 16384], P(None, None, 'gx', 'gy'), may hold values from -1 to 1
- probe_field: float32 [2, 256, 256], replicated, may hold values from -1 to 1
- propagator: bfloat16 [2, 256, 256], replicated
- measured: bfloat16 [2048, 256, 256], P(('gx', 'gy')), may hold values from 0 to 1
- counts: int32 [128], P(('gx', 'gy')), may hold values from 0 to 16, as said below
- offsets: int32 [2048, 2], P(('gx', 'gy')), may hold values from 0 to 2047, as said below
Outputs:
- object_grad: float32 [2, 2, 4096, 16384], P(None, None, 'gx', 'gy')
The draws below stay inside these ranges and needn't reach their ends.
Inputs may be any that keep to these rules, and one draw needn't show every extreme that they name: `counts`: the device half the gx axis away (same gy index) holds 16 live positions together with a device; some device holds 16. `offsets`: rows below 256, columns below 2048; on the last gx index rows are at most 0, on the last gy index columns at most 1792; slots at or beyond a device's count are unused.
All inputs are finite; a program needn't handle non-finite values.
Results may differ from the reference program's by a relative error of at most 0.012.
Values may be sent and summed in bfloat16 or wider, within the bound.
No kernel may reach another device: no remote copies, remote signals or barrier semaphores. Data moves between devices by JAX's collectives and lax.ppermute only.
A program may use at most 128 MiB of HBM per device.

```python
import jax
import jax.numpy as jnp
from jax import lax

WINDOW = 256
SLICES = 2
TILE_ROWS = 256
TILE_COLS = 2048
POS_DEV = 8
SLOT_DEV = 16
SLOTS = 2048
GX_HALF = 8
GY_COUNT = 8
ROWS = 4096
COLS = 16384


def draw_propagator(key, part):
    key = jax.random.fold_in(key, 37)
    noise = jax.random.normal(key, (2, WINDOW, WINDOW), jnp.float32)
    scales = jnp.array([0.64, 0.4], jnp.float32) / jnp.sqrt(jnp.float32(WINDOW))
    identity = jnp.eye(WINDOW, dtype=jnp.float32)
    diagonal = jnp.stack([0.8 * identity, 0.0 * identity], 0)
    return (noise * scales[:, None, None] + diagonal).astype(jnp.bfloat16)


def draw_counts(key, part):
    key = jax.random.fold_in(key, 11)
    lower = jax.random.randint(key, (GX_HALF, GY_COUNT), 0, 2 * POS_DEV + 1)
    lower = lower.at[0, 0].set(2 * POS_DEV)
    whole = jnp.concatenate([lower, 2 * POS_DEV - lower], 0)
    return whole.reshape(-1).astype(jnp.int32)


def draw_offsets(key, part):
    key = jax.random.fold_in(key, 23)
    row_key, col_key = jax.random.split(key)
    device_count = 2 * GX_HALF * GY_COUNT
    device = jnp.arange(device_count, dtype=jnp.int32)
    row_limit = jnp.where(device // GY_COUNT == 2 * GX_HALF - 1, TILE_ROWS - WINDOW + 1, TILE_ROWS)
    col_limit = jnp.where(device % GY_COUNT == GY_COUNT - 1, TILE_COLS - WINDOW + 1, TILE_COLS)
    rows = jax.random.randint(row_key, (device_count, SLOT_DEV), 0, row_limit[:, None])
    cols = jax.random.randint(col_key, (device_count, SLOT_DEV), 0, col_limit[:, None])
    corners = jnp.stack([rows, cols], -1).reshape(device_count * SLOT_DEV, 2)
    corners = corners.at[0].set(jnp.array([TILE_ROWS - 1, TILE_COLS - 1], jnp.int32))
    corners = corners.at[1].set(jnp.array([0, 0], jnp.int32))
    return corners.astype(jnp.int32)


def block_levels(own_key, extent, cuts, least, high):
    factor_of, own = 1.0, jax.random.fold_in(own_key, 6)
    for dim, blocks in cuts:
        draws = jnp.exp(jax.random.uniform(jax.random.fold_in(own, dim), (blocks,), jnp.float32, least / len(cuts), high / len(cuts)))
        factor_of = factor_of * jnp.repeat(draws, extent[dim] // blocks).reshape([-1 if axis == dim else 1 for axis in range(len(extent))])
    return factor_of


def setup_inputs(seed: int = 0) -> dict:
    streams_of = jax.random.split(jax.random.key(seed), 7)
    object_field = jnp.clip(jax.random.uniform(streams_of[0], (SLICES, 2, ROWS, COLS), jnp.float32, -1.0, 1.0) * block_levels(streams_of[0], (SLICES, 2, ROWS, COLS), ((2, 16), (3, 8)), -0.4, 0.0), -1.0, 1.0).astype(jnp.bfloat16)
    probe_field = jnp.clip(jax.random.uniform(streams_of[1], (2, WINDOW, WINDOW), jnp.float32, -1.0, 1.0), -1.0, 1.0)
    propagator = draw_propagator(jax.random.fold_in(streams_of[6], 71), 0)
    measured = jnp.clip(1.0 * jax.random.uniform(streams_of[3], (SLOTS, WINDOW, WINDOW), jnp.float32) ** block_levels(streams_of[3], (SLOTS, WINDOW, WINDOW), ((0, 128),), -0.2, 0.2), 0.0, 1.0).astype(jnp.bfloat16)
    counts = draw_counts(jax.random.fold_in(streams_of[6], 71), 0)
    offsets = draw_offsets(jax.random.fold_in(streams_of[6], 71), 0)
    return {"object_field": object_field, "probe_field": probe_field, "propagator": propagator, "measured": measured, "counts": counts, "offsets": offsets}


LEFT_FORM = "ik,bkj->bij"
RIGHT_FORM = "bik,jk->bij"
ADJOINT_LEFT = "ki,bkj->bij"
ADJOINT_RIGHT = "bik,kj->bij"


def complex_product(pattern, first_real, first_imag, second_real, second_imag):
    def product(first, second):
        return jnp.einsum(pattern, first.astype(jnp.float32), second.astype(jnp.float32))
    real_part = product(first_real, second_real) - product(first_imag, second_imag)
    imag_part = product(first_real, second_imag) + product(first_imag, second_real)
    return real_part, imag_part


def patch_gradient(windows, probe_field, propagator, measured):
    batch_size = windows.shape[0]
    prop_real = propagator[0]
    prop_imag = propagator[1]
    conj_imag = -propagator[1]
    wave_real = jnp.broadcast_to(probe_field[0], (batch_size,) + probe_field.shape[1:])
    wave_imag = jnp.broadcast_to(probe_field[1], (batch_size,) + probe_field.shape[1:])
    incident_waves = []
    for slice_index in range(SLICES):
        obj_real = windows[:, slice_index, 0].astype(jnp.float32)
        obj_imag = windows[:, slice_index, 1].astype(jnp.float32)
        incident_waves.append((wave_real, wave_imag))
        lit_real = (wave_real * obj_real - wave_imag * obj_imag).astype(jnp.bfloat16)
        lit_imag = (wave_real * obj_imag + wave_imag * obj_real).astype(jnp.bfloat16)
        half_real, half_imag = complex_product(LEFT_FORM, prop_real, prop_imag, lit_real, lit_imag)
        half_real = half_real.astype(jnp.bfloat16)
        half_imag = half_imag.astype(jnp.bfloat16)
        wave_real, wave_imag = complex_product(RIGHT_FORM, half_real, half_imag, prop_real, prop_imag)
    misfit = wave_real * wave_real + wave_imag * wave_imag - measured.astype(jnp.float32)
    back_real = (misfit * wave_real).astype(jnp.bfloat16)
    back_imag = (misfit * wave_imag).astype(jnp.bfloat16)
    slice_grads = []
    for slice_index in reversed(range(SLICES)):
        half_real, half_imag = complex_product(ADJOINT_LEFT, prop_real, conj_imag, back_real, back_imag)
        half_real = half_real.astype(jnp.bfloat16)
        half_imag = half_imag.astype(jnp.bfloat16)
        lit_real, lit_imag = complex_product(ADJOINT_RIGHT, half_real, half_imag, prop_real, conj_imag)
        incident_real, incident_imag = incident_waves[slice_index]
        slice_grads.insert(0, jnp.stack([incident_real * lit_real + incident_imag * lit_imag,
                                         incident_real * lit_imag - incident_imag * lit_real], 1).astype(jnp.bfloat16))
        if slice_index > 0:
            obj_real = windows[:, slice_index, 0].astype(jnp.float32)
            obj_imag = windows[:, slice_index, 1].astype(jnp.float32)
            back_real = (obj_real * lit_real + obj_imag * lit_imag).astype(jnp.bfloat16)
            back_imag = (obj_real * lit_imag - obj_imag * lit_real).astype(jnp.bfloat16)
    return jnp.stack(slice_grads, 1)


def reference(object_field, probe_field, propagator, measured, counts, offsets):
    zero_index = jnp.zeros((), jnp.int32)

    def visit(position, gradient):
        position = jnp.asarray(position).astype(jnp.int32)
        device = position // SLOT_DEV
        in_use = (position % SLOT_DEV) < counts[device]
        row_start = ((device // GY_COUNT) * TILE_ROWS + offsets[position, 0]).astype(jnp.int32)
        col_start = ((device % GY_COUNT) * TILE_COLS + offsets[position, 1]).astype(jnp.int32)
        corner = (zero_index, zero_index, row_start, col_start)

        def accumulate(gradient):
            windows = lax.dynamic_slice(object_field, corner, (SLICES, 2, WINDOW, WINDOW))[None]
            intensity = lax.dynamic_slice_in_dim(measured, position, 1, 0)
            patch = patch_gradient(windows, probe_field, propagator, intensity)[0]
            previous = lax.dynamic_slice(gradient, corner, (SLICES, 2, WINDOW, WINDOW))
            return lax.dynamic_update_slice(gradient, previous + patch.astype(jnp.float32), corner)

        def keep_same(gradient):
            return gradient

        return lax.cond(in_use, accumulate, keep_same, gradient)

    return lax.fori_loop(0, SLOTS, visit, jnp.zeros(object_field.shape, jnp.float32))
```

```python
import functools

import jax
import jax.numpy as jnp
from jax import lax
from jax.experimental import pallas as pl
from jax.experimental.pallas import tpu as pltpu
from jax.sharding import PartitionSpec as P

LANE = 128
WIN = 256
COLS = 2048
PLANES = 4
SLOTS = 16
TILES = (COLS + WIN) // LANE
IN_CUTS = (0, 256, 640, 896, 1152, 1408, 1664, 1920, 2048)
GROUP_CUTS = (0, 384, 640, 896, 1152, 1408, 1664, 2048)
LAG = 2
VMEM_BYTES = 16 * 1024 * 1024
F32, BF16 = jnp.float32, jnp.bfloat16

SMEM_SPEC = pl.BlockSpec(memory_space=pltpu.SMEM)
VMEM_SPEC = pl.BlockSpec(memory_space=pltpu.VMEM)
HBM_SPEC = pl.BlockSpec(memory_space=pl.ANY)


def shifted(x, axis, by):
    size = lax.axis_size(axis)
    pairs = [(i, i + by) for i in range(size) if 0 <= i + by < size]
    return lax.ppermute(x, axis, pairs)


def params():
    return pltpu.CompilerParams(vmem_limit_bytes=VMEM_BYTES)


def rows_loop(count, step, body):
    def one(index, _):
        body(pl.ds(pl.multiple_of(index * step, step), step), index * step)
        return 0

    lax.fori_loop(0, count // step, one, 0)


def widen(buffer, field, first, width, row_base):
    def some(rows, at):
        target = pl.ds(pl.multiple_of(row_base + at, 64), 64)
        for plane in range(PLANES):
            for tile in range(width // LANE):
                field[plane, first // LANE + tile, target, :] = buffer[
                    plane, rows, tile * LANE : (tile + 1) * LANE].astype(F32)

    rows_loop(WIN, 64, some)


def start_kernel(own, measured, left_in, right_in, probe_in, field, total, intensity, left, right,
                 probe, buffer, sems):
    small = [pltpu.make_async_copy(src, dst, sems.at[2 + at]) for at, (src, dst) in enumerate(
        [(measured, intensity), (left_in, left), (right_in, right), (probe_in, probe)])]
    chunk = 256

    def fetch(at):
        return pltpu.make_async_copy(own.at[:, :, pl.ds(at * chunk, chunk)], buffer.at[at % 2],
                                     sems.at[at % 2])

    fetch(0).start()
    for copy in small:
        copy.start()

    def clear(tile, _):
        total[:, tile] = jnp.zeros((PLANES, 2 * WIN, LANE), F32)
        return 0

    lax.fori_loop(0, TILES, clear, 0)
    for at in range(COLS // chunk):
        if (at + 1) * chunk < COLS:
            fetch(at + 1).start()
        fetch(at).wait()
        widen(buffer.at[at % 2], field, at * chunk, chunk, 0)
    for copy in small:
        copy.wait()


def process(chosen, start_col, offsets, field, total, intensity, left_form, right_form, probe, chi,
            half, wave1):
    places = []
    for index in chosen:
        row, col = offsets[index, 0], offsets[index, 1]
        tile = col // LANE
        shift = col - tile * LANE
        places.append((pl.ds(row, WIN), tile, shift, lax.rem(WIN + LANE - shift, WIN + LANE)))
    count = len(chosen)
    spread = range(WIN // LANE + 1)
    span = [slice(k * WIN, (k + 1) * WIN) for k in range(2)]

    def dot(a, b):
        return jnp.dot(a, b, preferred_element_type=F32)

    def window(k, plane):
        rows, tile, _, back = places[k]
        wide = jnp.concatenate([field[plane, tile + j, rows, :] for j in spread], 1)
        return pltpu.roll(wide, back, 1)[:, :WIN]

    def deposit(k, plane, value):
        rows, tile, shift, _ = places[k]
        value = value.astype(BF16).astype(F32)
        wide = jnp.concatenate([value, jnp.zeros((WIN, LANE), F32)], 1)
        wide = pltpu.roll(wide, shift, 1)
        for j in spread:
            total[plane, tile + j, rows, :] += wide[:, j * LANE : (j + 1) * LANE]

    def stack(k, real, imag):
        chi[span[0], span[k]] = real.astype(BF16)
        chi[span[1], span[k]] = imag.astype(BF16)

    def through(first, second):
        middle = dot(first[...], chi[:, : count * WIN]).astype(BF16)
        for k in range(count):
            for part in range(2):
                half[span[k], span[part]] = middle[span[part], span[k]]
        return dot(half[: count * WIN, :], second[...])

    for k in range(count):
        obj_real, obj_imag = window(k, 0), window(k, 1)
        stack(k, probe[0] * obj_real - probe[1] * obj_imag,
              probe[0] * obj_imag + probe[1] * obj_real)
    wave1[: count * WIN, :] = through(left_form, right_form)
    for k in range(count):
        obj_real, obj_imag = window(k, 2), window(k, 3)
        real, imag = wave1[span[k], span[0]], wave1[span[k], span[1]]
        stack(k, real * obj_real - imag * obj_imag, real * obj_imag + imag * obj_real)
    wave = through(left_form, right_form)
    for k in range(count):
        real, imag = wave[span[k], span[0]], wave[span[k], span[1]]
        misfit = real * real + imag * imag - intensity[chosen[k]].astype(F32)
        stack(k, misfit * real, misfit * imag)
    lit = through(right_form, left_form)
    for k in range(count):
        lit_real, lit_imag = lit[span[k], span[0]], lit[span[k], span[1]]
        obj_real, obj_imag = window(k, 2), window(k, 3)
        stack(k, obj_real * lit_real + obj_imag * lit_imag,
              obj_real * lit_imag - obj_imag * lit_real)
        real, imag = wave1[span[k], span[0]], wave1[span[k], span[1]]
        deposit(k, 2, real * lit_real + imag * lit_imag)
        deposit(k, 3, real * lit_imag - imag * lit_real)
    lit = through(right_form, left_form)
    for k in range(count):
        lit_real, lit_imag = lit[span[k], span[0]], lit[span[k], span[1]]
        deposit(k, 0, probe[0] * lit_real + probe[1] * lit_imag)
        deposit(k, 1, probe[0] * lit_imag - probe[1] * lit_real)


def step_kernel(plan, *refs):
    refs = list(refs)

    def take(count):
        taken = refs[:count]
        del refs[:count]
        return taken

    if plan["group"]:
        counts, offsets = take(2)
        intensity, left_form, right_form, probe = take(4)
    fresh = take(len(plan["fresh"]))
    landed = take(len(plan["landed"]))
    side = take(1) if plan["mix"] else None
    take(2)
    if plan["has_out"]:
        take(1)
    field, total = take(2)
    if plan["landed"]:
        (out,) = take(1)
    gives = take(len(plan["gives"]))
    placed, out_sems = take(2)
    if plan["group"]:
        chi, half, wave1, members = take(4)

    if plan["group"]:
        start, stop = plan["group"]

        def collect(index, found):
            col = offsets[index, 1]
            inside = (index < counts[0]) & (col >= start) & (col < stop)

            @pl.when(inside)
            def _():
                members[found] = index

            return found + inside.astype(jnp.int32)

        found = lax.fori_loop(0, SLOTS, collect, 0)

    for at, (first, width, row_base) in enumerate(plan["fresh"]):
        widen(fresh[at], field, first, width, row_base)

    if plan["group"]:
        static = (offsets, field, total, intensity, left_form, right_form, probe, chi, half, wave1)

        def pair(index, _):
            process([members[2 * index], members[2 * index + 1]], start, *static)
            return 0

        lax.fori_loop(0, found // 2, pair, 0)

        @pl.when(found % 2 == 1)
        def _():
            process([members[found - 1]], start, *static)

    sends = []
    for at, (first, width, row_base) in enumerate(plan["gives"]):
        add_side = plan["mix"]

        def narrow(rows, offset):
            source = pl.ds(pl.multiple_of(row_base + offset, 64), 64)
            for plane in range(PLANES):
                for tile in range(width // LANE):
                    cols = slice(tile * LANE, (tile + 1) * LANE)
                    value = total[plane, first // LANE + tile, source, :]
                    if add_side:
                        value = value + side[0][plane, rows, cols].astype(F32)
                    gives[at][plane, rows, cols] = value.astype(BF16)

        rows_loop(WIN, 64, narrow)

    groups = {}
    for at, (first, width) in enumerate(plan["landed"]):
        groups.setdefault((first, width), []).append(at)
    done = 0
    for (first, width), members_at in groups.items():

        def add(rows, offset):
            for plane in range(PLANES):
                for tile in range(width // LANE):
                    cols = slice(tile * LANE, (tile + 1) * LANE)
                    value = total[plane, first // LANE + tile, rows, :]
                    for at in members_at:
                        value = value + landed[at][plane, rows, cols].astype(F32)
                    placed[done, plane, rows, cols] = value

        rows_loop(WIN, 64, add)
        sends.append(pltpu.make_async_copy(placed.at[done, :, :, pl.ds(0, width)],
                                           out.at[:, :, pl.ds(first, width)],
                                           out_sems.at[len(sends)]))
        sends[-1].start()
        done += 1
    for copy in sends:
        copy.wait()


class Chain:
    def __init__(self, own, probe, propagator, measured, counts, offsets):
        real, imag = propagator[0], propagator[1]
        left_form = jnp.concatenate(
            [jnp.concatenate([real, -imag], 1), jnp.concatenate([imag, real], 1)], 0)
        self.counts, self.offsets, self.out = counts, offsets, None
        shapes = [((PLANES, TILES, 2 * WIN, LANE), F32)] * 2 + [
            (measured.shape, BF16), (left_form.shape, BF16), (left_form.shape, BF16),
            (probe.shape, F32)]
        made = pl.pallas_call(
            start_kernel,
            out_shape=[pltpu.VMEM(*shape) for shape in shapes],
            in_specs=[HBM_SPEC] * 5,
            out_specs=[VMEM_SPEC] * 6,
            scratch_shapes=[pltpu.VMEM((2, PLANES, WIN, 256), BF16), pltpu.SemaphoreType.DMA((6,))],
            compiler_params=params(),
            cost_estimate=pl.CostEstimate(flops=2**20, bytes_accessed=2**20, transcendentals=0),
            name="begin",
        )(own, measured, left_form, left_form.T, probe)
        self.field, self.total = made[:2]
        self.constants = made[2:]

    def step(self, group=None, fresh=(), landed=(), gives=(), mix=None):
        plan = {
            "group": group,
            "fresh": [(first, x.shape[2], row) for first, row, x in fresh],
            "landed": [(first, x.shape[2]) for first, x in landed],
            "gives": list(gives),
            "mix": mix is not None,
            "has_out": self.out is not None and len(landed) > 0,
        }
        args, specs = [], []
        if group:
            args += [self.counts, self.offsets, *self.constants]
            specs += [SMEM_SPEC] * 2 + [VMEM_SPEC] * 4
        args += [x for _, _, x in fresh] + [x for _, x in landed]
        specs += [VMEM_SPEC] * (len(fresh) + len(landed))
        if mix is not None:
            args.append(mix)
            specs.append(VMEM_SPEC)
        alias = {len(args): 0, len(args) + 1: 1}
        args += [self.field, self.total]
        specs += [VMEM_SPEC] * 2
        outs = [pltpu.VMEM(self.field.shape, F32), pltpu.VMEM(self.total.shape, F32)]
        out_specs = [VMEM_SPEC] * 2
        if landed:
            if self.out is not None:
                alias[len(args)] = 2
                args.append(self.out)
                specs.append(HBM_SPEC)
            outs.append(jax.ShapeDtypeStruct((PLANES, WIN, COLS), F32))
            out_specs.append(HBM_SPEC)
        outs += [jax.ShapeDtypeStruct((PLANES, WIN, width), BF16) for _, width, _ in gives]
        out_specs += [VMEM_SPEC] * len(gives)

        def widest(widths):
            return max([LANE, *widths])

        placed = len({first for first, _ in landed})
        scratch = [
            pltpu.VMEM((max(1, placed), PLANES, WIN, widest(x.shape[2] for _, x in landed)), F32),
            pltpu.SemaphoreType.DMA((max(1, placed),)),
        ]
        if group:
            scratch += [pltpu.VMEM((2 * WIN, 2 * WIN), BF16), pltpu.VMEM((2 * WIN, 2 * WIN), BF16),
                        pltpu.VMEM((2 * WIN, 2 * WIN), F32), pltpu.SMEM((SLOTS,), jnp.int32)]
        result = pl.pallas_call(
            functools.partial(step_kernel, plan),
            out_shape=outs,
            in_specs=specs,
            out_specs=out_specs,
            scratch_shapes=scratch,
            input_output_aliases=alias,
            compiler_params=params(),
            cost_estimate=pl.CostEstimate(flops=2**20, bytes_accessed=2**20, transcendentals=0),
            name="group" if group else "place",
        )(*args)
        self.field, self.total = result[:2]
        rest = list(result[2:])
        if landed:
            self.out = rest.pop(0)
        return rest


def body(object_field, probe_field, propagator, measured, counts, offsets):
    own = object_field.reshape(PLANES, WIN, COLS)
    lows = []
    for first, end in zip(IN_CUTS[:-1], IN_CUTS[1:]):
        lows.append((first, end, shifted(own[:, :, first:end], "gx", -1)))
    side_own = shifted(own[:, :, :WIN], "gy", -1)
    side_low = shifted(lows[0][2], "gy", -1)
    chain = Chain(own, probe_field, propagator, measured, counts, offsets)

    groups = list(zip(GROUP_CUTS[:-1], GROUP_CUTS[1:]))
    spills = []
    taken = 0
    for number, (start, stop) in enumerate(groups):
        final = number == len(groups) - 1
        fresh = []
        while taken < len(lows) and lows[taken][0] < stop + WIN:
            fresh.append((lows[taken][0], WIN, lows[taken][2]))
            taken += 1
        if number == 2:
            fresh.append((COLS, 0, side_own))
        if number == 3:
            fresh.append((COLS, WIN, side_low))
        landed = [spills[number - LAG]] if number >= LAG else []
        first = WIN if number == 0 else start
        gives = [(first, stop - first, WIN)]
        if final:
            gives = [(COLS, WIN, WIN)] + gives + [(COLS, WIN, 0)]
        given = chain.step((start, stop), fresh, landed, gives)
        if final:
            side_low_spill = shifted(given[0], "gy", 1)
            spills.append((first, shifted(given[1], "gx", 1)))
            side_own_spill = shifted(given[2], "gy", 1)
        else:
            spills.append((first, shifted(given[0], "gx", 1)))
    (first_spill,) = chain.step(None, [], [], [(0, WIN, WIN)], side_low_spill)
    first_spill = shifted(first_spill, "gx", 1)
    for spill in spills[len(groups) - LAG :]:
        chain.step(None, [], [spill])
    chain.step(None, [], [(0, first_spill), (0, side_own_spill)])
    return chain.out.reshape(object_field.shape)


def solution(mesh):
    in_specs = (
        P(None, None, "gx", "gy"),
        P(),
        P(),
        P(("gx", "gy"), None, None),
        P(("gx", "gy")),
        P(("gx", "gy"), None),
    )
    out_specs = P(None, None, "gx", "gy")
    return jax.shard_map(body, mesh=mesh, in_specs=in_specs, out_specs=out_specs, check_vma=False)
```

```python
import functools

import jax
import jax.numpy as jnp
from jax import lax
from jax.experimental import pallas as pl
from jax.experimental.pallas import tpu as pltpu
from jax.sharding import PartitionSpec as P

LANE = 128
WIN = 256
COLS = 2048
SLICES = 2
PLANES = 2 * SLICES
SLOTS = 16
TILES = (COLS + WIN) // LANE
IN_CUTS = (0, 512, 768, 1152, 1536, 1920, 2048)
GROUP_CUTS = (0, 256, 512, 896, 1280, 1664, 2048)
LAG = 2
BATCHES = (2, 1)
VMEM_BYTES = 16 * 1024 * 1024
F32, BF16 = jnp.float32, jnp.bfloat16

SMEM_SPEC = pl.BlockSpec(memory_space=pltpu.SMEM)
VMEM_SPEC = pl.BlockSpec(memory_space=pltpu.VMEM)
HBM_SPEC = pl.BlockSpec(memory_space=pl.ANY)


def shifted(x, axis, by):
    size = lax.axis_size(axis)
    pairs = [(i, i + by) for i in range(size) if 0 <= i + by < size]
    return lax.ppermute(x, axis, pairs)


def params():
    return pltpu.CompilerParams(vmem_limit_bytes=VMEM_BYTES)


def rows_loop(count, step, body):
    def one(index, _):
        body(pl.ds(pl.multiple_of(index * step, step), step), index * step)
        return 0

    lax.fori_loop(0, count // step, one, 0)


def widen(buffer, field, first, width, row_base):
    def some(rows, at):
        target = pl.ds(pl.multiple_of(row_base + at, 64), 64)
        for plane in range(PLANES):
            for tile in range(width // LANE):
                field[plane, first // LANE + tile, target, :] = buffer[
                    plane, rows, tile * LANE : (tile + 1) * LANE].astype(F32)

    rows_loop(WIN, 64, some)


def start_kernel(own, measured, left_in, right_in, probe_in, field, total, intensity, left, right,
                 probe, buffer, sems):
    small = [pltpu.make_async_copy(src, dst, sems.at[2 + at]) for at, (src, dst) in enumerate(
        [(measured, intensity), (left_in, left), (right_in, right), (probe_in, probe)])]
    chunk = 256

    def fetch(at):
        return pltpu.make_async_copy(own.at[:, :, pl.ds(at * chunk, chunk)], buffer.at[at % 2],
                                     sems.at[at % 2])

    fetch(0).start()
    for copy in small:
        copy.start()

    def clear(tile, _):
        total[:, tile] = jnp.zeros((PLANES, 2 * WIN, LANE), F32)
        return 0

    lax.fori_loop(0, TILES, clear, 0)

    for at in range(COLS // chunk):
        if (at + 1) * chunk < COLS:
            fetch(at + 1).start()
        fetch(at).wait()
        widen(buffer.at[at % 2], field, at * chunk, chunk, 0)
    for copy in small:
        copy.wait()


def process(chosen, offsets, field, total, intensity, left_form, right_form, probe_ref, chi,
            half, waves):
    places = []
    for index in chosen:
        row, col = offsets[2 * index], offsets[2 * index + 1]
        tile = col // LANE
        shift = col - tile * LANE
        places.append((pl.ds(row, WIN), tile, shift, lax.rem(WIN + LANE - shift, WIN + LANE)))
    count = len(chosen)
    probe = (probe_ref[0], probe_ref[1])
    spread = range(WIN // LANE + 1)
    span = (slice(0, WIN), slice(WIN, 2 * WIN))

    def dot(a, b):
        return jnp.dot(a, b, preferred_element_type=F32)

    def window(k, plane):
        rows, tile, _, back = places[k]
        wide = jnp.concatenate([field[plane, tile + j, rows, :] for j in spread], 1)
        return pltpu.roll(wide, back, 1)[:, :WIN]

    def deposit(k, plane, value):
        rows, tile, shift, _ = places[k]
        value = value.astype(BF16).astype(F32)
        wide = jnp.concatenate([value, jnp.zeros((WIN, LANE), F32)], 1)
        wide = pltpu.roll(wide, shift, 1)
        for j in spread:
            total[plane, tile + j, rows, :] += wide[:, j * LANE : (j + 1) * LANE]

    def stack(k, real, imag):
        chi[k, span[0], :] = real.astype(BF16)
        chi[k, span[1], :] = imag.astype(BF16)

    def through(k, first, second):
        middle = dot(first[...], chi[k]).astype(BF16)
        for part in range(2):
            half[k, :, span[part]] = middle[span[part]]
        result = dot(half[k], second[...])
        return result[:, span[0]], result[:, span[1]]

    for level in range(SLICES):
        for k in range(count):
            obj_real, obj_imag = window(k, 2 * level), window(k, 2 * level + 1)
            real, imag = (waves[k, level - 1, 0], waves[k, level - 1, 1]) if level else probe
            stack(k, real * obj_real - imag * obj_imag, real * obj_imag + imag * obj_real)
        for k in range(count):
            real, imag = through(k, left_form, right_form)
            if level < SLICES - 1:
                waves[k, level, 0] = real
                waves[k, level, 1] = imag
            else:
                misfit = real * real + imag * imag - intensity[chosen[k]].astype(F32)
                stack(k, misfit * real, misfit * imag)
    for level in reversed(range(SLICES)):
        for k in range(count):
            lit_real, lit_imag = through(k, right_form, left_form)
            if level:
                obj_real, obj_imag = window(k, 2 * level), window(k, 2 * level + 1)
                stack(k, obj_real * lit_real + obj_imag * lit_imag,
                      obj_real * lit_imag - obj_imag * lit_real)
            real, imag = (waves[k, level - 1, 0], waves[k, level - 1, 1]) if level else probe
            deposit(k, 2 * level, real * lit_real + imag * lit_imag)
            deposit(k, 2 * level + 1, real * lit_imag - imag * lit_real)


def step_kernel(plan, *refs):
    refs = list(refs)

    def take(count):
        taken = refs[:count]
        del refs[:count]
        return taken

    if plan["number"] is not None:
        counts, offsets = take(2)
        intensity, left_form, right_form, probe = take(4)
    fresh = take(len(plan["fresh"]))
    landed = take(len(plan["landed"]))
    side = take(1) if plan["mix"] else None
    take(2)
    if plan["has_out"]:
        take(1)
    field, total = take(2)
    if plan["landed"]:
        (out,) = take(1)
    gives = take(len(plan["gives"]))
    placed, out_sems = take(2)
    if plan["number"] is not None:
        chi, half, waves, members = take(4)

    for at, (first, width, row_base) in enumerate(plan["fresh"]):
        widen(fresh[at], field, first, width, row_base)

    if plan["number"] is not None:
        static = (offsets, field, total, intensity, left_form, right_form, probe, chi, half,
                  waves)
        start, stop = GROUP_CUTS[plan["number"]], GROUP_CUTS[plan["number"] + 1]

        def collect(index, found):
            col = offsets[2 * index + 1]
            inside = (index < counts[0]) & (col >= start) & (col < stop)

            @pl.when(inside)
            def _():
                members[found] = index

            return found + inside.astype(jnp.int32)

        found = lax.fori_loop(0, SLOTS, collect, 0)
        at = 0
        for size in BATCHES:

            def batch(index, first, size=size):
                process([members[first + k] for k in range(size)], *static)
                return first + size

            at = lax.fori_loop(0, (found - at) // size, batch, at)

    sends = []
    for at, (first, width, row_base) in enumerate(plan["gives"]):
        add_side = plan["mix"]

        def narrow(rows, offset):
            source = pl.ds(pl.multiple_of(row_base + offset, 64), 64)
            for plane in range(PLANES):
                for tile in range(width // LANE):
                    cols = slice(tile * LANE, (tile + 1) * LANE)
                    value = total[plane, first // LANE + tile, source, :]
                    if add_side:
                        value = value + side[0][plane, rows, cols].astype(F32)
                    gives[at][plane, rows, cols] = value.astype(BF16)

        rows_loop(WIN, 64, narrow)

    groups = {}
    for at, (first, width) in enumerate(plan["landed"]):
        groups.setdefault((first, width), []).append(at)
    done = 0
    for (first, width), members_at in groups.items():

        def add(rows, offset):
            for plane in range(PLANES):
                for tile in range(width // LANE):
                    cols = slice(tile * LANE, (tile + 1) * LANE)
                    value = total[plane, first // LANE + tile, rows, :]
                    for at in members_at:
                        value = value + landed[at][plane, rows, cols].astype(F32)
                    placed[done, plane, rows, cols] = value

        rows_loop(WIN, 64, add)
        sends.append(pltpu.make_async_copy(placed.at[done, :, :, pl.ds(0, width)],
                                           out.at[:, :, pl.ds(first, width)],
                                           out_sems.at[len(sends)]))
        sends[-1].start()
        done += 1
    for copy in sends:
        copy.wait()


class Chain:
    def __init__(self, own, probe, propagator, measured, counts, offsets):
        real, imag = propagator[0], propagator[1]
        left_form = jnp.concatenate(
            [jnp.concatenate([real, -imag], 1), jnp.concatenate([imag, real], 1)], 0)
        self.counts, self.offsets, self.out = counts, offsets.reshape(-1), None
        shapes = [((PLANES, TILES, 2 * WIN, LANE), F32)] * 2 + [
            (measured.shape, BF16), (left_form.shape, BF16), (left_form.shape, BF16),
            (probe.shape, F32)]
        made = pl.pallas_call(
            start_kernel,
            out_shape=[pltpu.VMEM(*shape) for shape in shapes],
            in_specs=[HBM_SPEC] * 5,
            out_specs=[VMEM_SPEC] * 6,
            scratch_shapes=[pltpu.VMEM((2, PLANES, WIN, 256), BF16), pltpu.SemaphoreType.DMA((6,))],
            compiler_params=params(),
            cost_estimate=pl.CostEstimate(flops=2**20, bytes_accessed=2**20, transcendentals=0),
            name="begin",
        )(own, measured, left_form, left_form.T, probe)
        self.field, self.total = made[:2]
        self.constants = made[2:]

    def step(self, number=None, fresh=(), landed=(), gives=(), mix=None):
        plan = {
            "number": number,
            "fresh": [(first, x.shape[2], row) for first, row, x in fresh],
            "landed": [(first, x.shape[2]) for first, x in landed],
            "gives": list(gives),
            "mix": mix is not None,
            "has_out": self.out is not None and len(landed) > 0,
        }
        args, specs = [], []
        if number is not None:
            args += [self.counts, self.offsets, *self.constants]
            specs += [SMEM_SPEC] * 2 + [VMEM_SPEC] * 4
        args += [x for _, _, x in fresh] + [x for _, x in landed]
        specs += [VMEM_SPEC] * (len(fresh) + len(landed))
        if mix is not None:
            args.append(mix)
            specs.append(VMEM_SPEC)
        alias = {len(args): 0, len(args) + 1: 1}
        args += [self.field, self.total]
        specs += [VMEM_SPEC] * 2
        outs = [pltpu.VMEM(self.field.shape, F32), pltpu.VMEM(self.total.shape, F32)]
        out_specs = [VMEM_SPEC] * 2
        if landed:
            if self.out is not None:
                alias[len(args)] = 2
                args.append(self.out)
                specs.append(HBM_SPEC)
            outs.append(jax.ShapeDtypeStruct((PLANES, WIN, COLS), F32))
            out_specs.append(HBM_SPEC)
        outs += [jax.ShapeDtypeStruct((PLANES, WIN, width), BF16) for _, width, _ in gives]
        out_specs += [VMEM_SPEC] * len(gives)

        def widest(widths):
            return max([LANE, *widths])

        placed = len({first for first, _ in landed})
        scratch = [
            pltpu.VMEM((max(1, placed), PLANES, WIN, widest(x.shape[2] for _, x in landed)), F32),
            pltpu.SemaphoreType.DMA((max(1, placed),)),
        ]
        if number is not None:
            most = BATCHES[0]
            scratch += [pltpu.VMEM((most, 2 * WIN, WIN), BF16),
                        pltpu.VMEM((most, WIN, 2 * WIN), BF16),
                        pltpu.VMEM((most, SLICES - 1, 2, WIN, WIN), F32),
                        pltpu.SMEM((SLOTS,), jnp.int32)]
        result = pl.pallas_call(
            functools.partial(step_kernel, plan),
            out_shape=outs,
            in_specs=specs,
            out_specs=out_specs,
            scratch_shapes=scratch,
            input_output_aliases=alias,
            compiler_params=params(),
            cost_estimate=pl.CostEstimate(flops=2**20, bytes_accessed=2**20, transcendentals=0),
            name="place" if number is None else "group",
        )(*args)
        self.field, self.total = result[:2]
        rest = list(result[2:])
        if landed:
            self.out = rest.pop(0)
        return rest


def body(object_field, probe_field, propagator, measured, counts, offsets):
    own = object_field.reshape(PLANES, WIN, COLS)
    lows = []
    for first, end in zip(IN_CUTS[:-1], IN_CUTS[1:]):
        lows.append((first, end, shifted(own[:, :, first:end], "gx", -1)))
    side_own = shifted(own[:, :, :WIN], "gy", -1)
    side_low = shifted(lows[0][2][:, :, :WIN], "gy", -1)
    chain = Chain(own, probe_field, propagator, measured, counts, offsets)

    groups = list(zip(GROUP_CUTS[:-1], GROUP_CUTS[1:]))
    spills, placed = [], 0
    taken = 0
    for number, (start, stop) in enumerate(groups):
        final = number == len(groups) - 1
        fresh = []
        while taken < len(lows) and lows[taken][0] < stop + WIN:
            fresh.append((lows[taken][0], WIN, lows[taken][2]))
            taken += 1
        if number == 1:
            fresh.append((COLS, 0, side_own))
        if number == 3:
            fresh.append((COLS, WIN, side_low))
        landed = []
        if len(spills) - placed >= LAG:
            landed = [spills[placed]]
            placed += 1
        first = max(start, WIN)
        gives = [(first, stop - first, WIN)] if stop > first else []
        if final:
            gives = [(COLS, WIN, WIN)] + gives + [(COLS, WIN, 0)]
        given = chain.step(number, fresh, landed, gives)
        if final:
            side_low_spill = shifted(given[0], "gy", 1)
            spills.append((first, shifted(given[1], "gx", 1)))
            side_own_spill = shifted(given[2], "gy", 1)
        elif gives:
            spills.append((first, shifted(given[0], "gx", 1)))
    while placed < len(spills) - 1:
        chain.step(None, [], [spills[placed]])
        placed += 1
    (first_spill,) = chain.step(None, [], [], [(0, WIN, WIN)], side_low_spill)
    first_spill = shifted(first_spill, "gx", 1)
    for spill in spills[placed:]:
        chain.step(None, [], [spill])
    chain.step(None, [], [(0, first_spill), (0, side_own_spill)])
    return chain.out.reshape(object_field.shape)


def solution(mesh):
    in_specs = (
        P(None, None, "gx", "gy"),
        P(),
        P(),
        P(("gx", "gy"), None, None),
        P(("gx", "gy")),
        P(("gx", "gy"), None),
    )
    out_specs = P(None, None, "gx", "gy")
    return jax.shard_map(body, mesh=mesh, in_specs=in_specs, out_specs=out_specs, check_vma=False)
```

```python
import functools

import jax
import jax.numpy as jnp
from jax import lax
from jax.experimental import pallas as pl
from jax.experimental.pallas import tpu as pltpu
from jax.sharding import PartitionSpec as P

LANE = 128
WIN = 256
COLS = 2048
SLICES = 2
PLANES = 2 * SLICES
SLOTS = 16
TILES = (COLS + WIN) // LANE
RING = 8
KEPT = RING + WIN // LANE
IN_CUTS = (0, 512, 768, 1152, 1536, 1920, 2048)
GROUP_CUTS = (0, 256, 512, 896, 1280, 1664, 2048)
LAG = 2
BATCHES = (2, 1)
VMEM_BYTES = 8 * 1024 * 1024
F32, BF16 = jnp.float32, jnp.bfloat16

SMEM_SPEC = pl.BlockSpec(memory_space=pltpu.SMEM)
VMEM_SPEC = pl.BlockSpec(memory_space=pltpu.VMEM)
HBM_SPEC = pl.BlockSpec(memory_space=pl.ANY)


def shifted(x, axis, by):
    size = lax.axis_size(axis)
    pairs = [(i, i + by) for i in range(size) if 0 <= i + by < size]
    return lax.ppermute(x, axis, pairs)


def params():
    return pltpu.CompilerParams(vmem_limit_bytes=VMEM_BYTES)


def rows_loop(count, step, body):
    def one(index, _):
        body(pl.ds(pl.multiple_of(index * step, step), step), index * step)
        return 0

    lax.fori_loop(0, count // step, one, 0)


def widen(buffer, field, first, width, row_base):
    def some(rows, at):
        target = pl.ds(pl.multiple_of(row_base + at, 64), 64)
        for plane in range(PLANES):
            for tile in range(width // LANE):
                at_tile = first // LANE + tile
                place = at_tile % RING if first < COLS else at_tile - COLS // LANE + RING
                field[plane, place, target, :] = buffer[
                    plane, rows, tile * LANE : (tile + 1) * LANE].astype(F32)

    rows_loop(buffer.shape[1], 64, some)


def start_kernel(field, total):
    def clear(tile, _):
        total[:, tile] = jnp.zeros((PLANES, 2 * WIN, LANE), F32)
        return 0

    lax.fori_loop(0, TILES, clear, 0)
    field[0, 0, 0:8, :] = jnp.zeros((8, LANE), F32)


def process(chosen, offsets, field, total, intensity, left_form, right_form, probe_ref, chi,
            half, waves, kept):
    lane = lax.broadcasted_iota(jnp.int32, (WIN, LANE), 1)
    places = []
    for index in chosen:
        row, col = offsets[2 * index], offsets[2 * index + 1]
        tile = col // LANE
        shift = col - tile * LANE
        places.append((pl.ds(row, WIN), tile, shift))
    count = len(chosen)
    probe = (probe_ref[0], probe_ref[1])
    spread = WIN // LANE
    span = (slice(0, WIN), slice(WIN, 2 * WIN))

    def dot(a, b):
        return jnp.dot(a, b, preferred_element_type=F32)

    def window(k, plane):
        rows, tile, shift = places[k]
        back = lax.rem(LANE - shift, LANE)
        turned = []
        for j in range(spread + 1):
            at = tile + j
            place = jnp.where(at < COLS // LANE, lax.rem(at, RING), at - COLS // LANE + RING)
            turned.append(pltpu.roll(field[plane, place, rows, :], back, 1))
        return jnp.concatenate(
            [jnp.where(lane < LANE - shift, turned[j], turned[j + 1]) for j in range(spread)], 1)

    def deposit(k, plane, value):
        rows, tile, shift = places[k]
        turned = [pltpu.roll(value[:, j * LANE : (j + 1) * LANE], shift, 1) for j in range(spread)]
        inside = lane >= shift
        for j in range(spread + 1):
            if j == 0:
                part = jnp.where(inside, turned[0], 0.0)
            elif j == spread:
                part = jnp.where(inside, 0.0, turned[spread - 1])
            else:
                part = jnp.where(inside, turned[j], turned[j - 1])
            total[plane, tile + j, rows, :] += part

    def stack(k, real, imag):
        chi[k, span[0], :] = real.astype(BF16)
        chi[k, span[1], :] = imag.astype(BF16)

    def through(k, first, second):
        middle = dot(first[...], chi[k]).astype(BF16)
        for part in range(2):
            half[k, :, span[part]] = middle[span[part]]
        result = dot(half[k], second[...])
        return result[:, span[0]], result[:, span[1]]

    for level in range(SLICES):
        for k in range(count):
            obj_real, obj_imag = window(k, 2 * level), window(k, 2 * level + 1)
            if level:
                kept[k, level - 1, 0] = obj_real.astype(BF16)
                kept[k, level - 1, 1] = obj_imag.astype(BF16)
            real, imag = (waves[k, level - 1, 0], waves[k, level - 1, 1]) if level else probe
            stack(k, real * obj_real - imag * obj_imag, real * obj_imag + imag * obj_real)
        for k in range(count):
            real, imag = through(k, left_form, right_form)
            if level < SLICES - 1:
                waves[k, level, 0] = real
                waves[k, level, 1] = imag
            else:
                misfit = real * real + imag * imag - intensity[chosen[k]].astype(F32)
                stack(k, misfit * real, misfit * imag)
    for level in reversed(range(SLICES)):
        for k in range(count):
            lit_real, lit_imag = through(k, right_form, left_form)
            if level:
                obj_real = kept[k, level - 1, 0].astype(F32)
                obj_imag = kept[k, level - 1, 1].astype(F32)
                stack(k, obj_real * lit_real + obj_imag * lit_imag,
                      obj_real * lit_imag - obj_imag * lit_real)
            real, imag = (waves[k, level - 1, 0], waves[k, level - 1, 1]) if level else probe
            deposit(k, 2 * level, real * lit_real + imag * lit_imag)
            deposit(k, 2 * level + 1, real * lit_imag - imag * lit_real)


def step_kernel(plan, *refs):
    refs = list(refs)

    def take(count):
        taken = refs[:count]
        del refs[:count]
        return taken

    if plan["number"] is not None:
        counts, offsets = take(2)
        intensity, left_form, right_form, probe = take(4)
    fresh = take(len(plan["fresh"]))
    landed = take(len(plan["landed"]))
    side = take(1) if plan["mix"] else None
    take(2)
    if plan["has_out"]:
        take(1)
    field, total = take(2)
    if plan["landed"]:
        (out,) = take(1)
    gives = take(len(plan["gives"]))
    placed, out_sems = take(2)
    if plan["number"] is not None:
        chi, half, waves, kept, members = take(5)

    for at, (first, width, row_base) in enumerate(plan["fresh"]):
        widen(fresh[at], field, first, width, row_base)

    if plan["number"] is not None:
        static = (offsets, field, total, intensity, left_form, right_form, probe, chi, half,
                  waves, kept)
        start, stop = GROUP_CUTS[plan["number"]], GROUP_CUTS[plan["number"] + 1]

        def collect(index, found):
            col = offsets[2 * index + 1]
            inside = (index < counts[0]) & (col >= start) & (col < stop)

            @pl.when(inside)
            def _():
                members[found] = index

            return found + inside.astype(jnp.int32)

        found = lax.fori_loop(0, SLOTS, collect, 0)
        at = 0
        for size in BATCHES:

            def batch(index, first, size=size):
                process([members[first + k] for k in range(size)], *static)
                return first + size

            at = lax.fori_loop(0, (found - at) // size, batch, at)

    sends = []
    for at, (first, width, row_base) in enumerate(plan["gives"]):
        add_side = plan["mix"]

        def narrow(rows, offset):
            source = pl.ds(pl.multiple_of(row_base + offset, 64), 64)
            for plane in range(PLANES):
                for tile in range(width // LANE):
                    cols = slice(tile * LANE, (tile + 1) * LANE)
                    value = total[plane, first // LANE + tile, source, :]
                    if add_side:
                        value = value + side[0][plane, rows, cols].astype(F32)
                    gives[at][plane, rows, cols] = value.astype(BF16)

        rows_loop(WIN, 64, narrow)

    groups = {}
    for at, (first, width) in enumerate(plan["landed"]):
        groups.setdefault((first, width), []).append(at)
    done = 0
    for (first, width), members_at in groups.items():

        def add(rows, offset):
            for plane in range(PLANES):
                for tile in range(width // LANE):
                    cols = slice(tile * LANE, (tile + 1) * LANE)
                    value = total[plane, first // LANE + tile, rows, :]
                    for at in members_at:
                        value = value + landed[at][plane, rows, cols].astype(F32)
                    placed[done, plane, rows, cols] = value

        rows_loop(WIN, 64, add)
        sends.append(pltpu.make_async_copy(placed.at[done, :, :, pl.ds(0, width)],
                                           out.at[:, :, pl.ds(first, width)],
                                           out_sems.at[len(sends)]))
        sends[-1].start()
        done += 1
    for copy in sends:
        copy.wait()


class Chain:
    def __init__(self, probe, propagator, measured, counts, offsets):
        real, imag = propagator[0], propagator[1]
        left_form = jnp.concatenate(
            [jnp.concatenate([real, -imag], 1), jnp.concatenate([imag, real], 1)], 0)
        self.counts, self.offsets, self.out = counts, offsets.reshape(-1), None
        self.constants = (measured, left_form, left_form.T, probe)
        self.field, self.total = pl.pallas_call(
            start_kernel,
            out_shape=[pltpu.VMEM((PLANES, KEPT, 2 * WIN, LANE), F32),
                       pltpu.VMEM((PLANES, TILES, 2 * WIN, LANE), F32)],
            out_specs=[VMEM_SPEC] * 2,
            compiler_params=params(),
            cost_estimate=pl.CostEstimate(flops=2**20, bytes_accessed=2**20, transcendentals=0),
            name="begin",
        )()

    def step(self, number=None, fresh=(), landed=(), gives=(), mix=None):
        plan = {
            "number": number,
            "fresh": [(first, x.shape[2], row) for first, row, x in fresh],
            "landed": [(first, x.shape[2]) for first, x in landed],
            "gives": list(gives),
            "mix": mix is not None,
            "has_out": self.out is not None and len(landed) > 0,
        }
        args, specs = [], []
        if number is not None:
            args += [self.counts, self.offsets, *self.constants]
            specs += [SMEM_SPEC] * 2 + [VMEM_SPEC] * 4
        args += [x for _, _, x in fresh] + [x for _, x in landed]
        specs += [VMEM_SPEC] * (len(fresh) + len(landed))
        if mix is not None:
            args.append(mix)
            specs.append(VMEM_SPEC)
        alias = {len(args): 0, len(args) + 1: 1}
        args += [self.field, self.total]
        specs += [VMEM_SPEC] * 2
        outs = [pltpu.VMEM(self.field.shape, F32), pltpu.VMEM(self.total.shape, F32)]
        out_specs = [VMEM_SPEC] * 2
        if landed:
            if self.out is not None:
                alias[len(args)] = 2
                args.append(self.out)
                specs.append(HBM_SPEC)
            outs.append(jax.ShapeDtypeStruct((PLANES, WIN, COLS), F32))
            out_specs.append(HBM_SPEC)
        outs += [jax.ShapeDtypeStruct((PLANES, WIN, width), BF16) for _, width, _ in gives]
        out_specs += [VMEM_SPEC] * len(gives)

        def widest(widths):
            return max([LANE, *widths])

        placed = len({first for first, _ in landed})
        scratch = [
            pltpu.VMEM((max(1, placed), PLANES, WIN, widest(x.shape[2] for _, x in landed)), F32),
            pltpu.SemaphoreType.DMA((max(1, placed),)),
        ]
        if number is not None:
            most = BATCHES[0]
            scratch += [pltpu.VMEM((most, 2 * WIN, WIN), BF16),
                        pltpu.VMEM((most, WIN, 2 * WIN), BF16),
                        pltpu.VMEM((most, SLICES - 1, 2, WIN, WIN), F32),
                        pltpu.VMEM((most, SLICES - 1, 2, WIN, WIN), BF16),
                        pltpu.SMEM((SLOTS,), jnp.int32)]
        result = pl.pallas_call(
            functools.partial(step_kernel, plan),
            out_shape=outs,
            in_specs=specs,
            out_specs=out_specs,
            scratch_shapes=scratch,
            input_output_aliases=alias,
            compiler_params=params(),
            cost_estimate=pl.CostEstimate(flops=2**20, bytes_accessed=2**20, transcendentals=0),
            name="place" if number is None else "group",
        )(*args)
        self.field, self.total = result[:2]
        rest = list(result[2:])
        if landed:
            self.out = rest.pop(0)
        return rest


def body(object_field, probe_field, propagator, measured, counts, offsets):
    own = object_field.reshape(PLANES, WIN, COLS)
    lows = []
    for first, end in zip(IN_CUTS[:-1], IN_CUTS[1:]):
        upper = own[:, :, first:end]
        lows.append((first, upper, shifted(upper, "gx", -1)))
    side_own = shifted(own[:, :, :WIN], "gy", -1)
    side_low = shifted(lows[0][2][:, :, :WIN], "gy", -1)
    chain = Chain(probe_field, propagator, measured, counts, offsets)

    groups = list(zip(GROUP_CUTS[:-1], GROUP_CUTS[1:]))
    spills, placed = [], 0
    taken = 0
    for number, (start, stop) in enumerate(groups):
        final = number == len(groups) - 1
        fresh = []
        while taken < len(lows) and lows[taken][0] < stop + WIN:
            fresh.append((lows[taken][0], 0, lows[taken][1]))
            fresh.append((lows[taken][0], WIN, lows[taken][2]))
            taken += 1
        if number == 1:
            fresh.append((COLS, 0, side_own))
        if number == 2:
            fresh.append((COLS, WIN, side_low))
        landed = []
        if len(spills) - placed >= LAG:
            landed = [spills[placed]]
            placed += 1
        first = max(start, WIN)
        gives = [(first, stop - first, WIN)] if stop > first else []
        if final:
            gives = [(COLS, WIN, WIN)] + gives + [(COLS, WIN, 0)]
        given = chain.step(number, fresh, landed, gives)
        if final:
            side_low_spill = shifted(given[0], "gy", 1)
            spills.append((first, shifted(given[1], "gx", 1)))
            side_own_spill = shifted(given[2], "gy", 1)
        elif gives:
            spills.append((first, shifted(given[0], "gx", 1)))
    while placed < len(spills) - 1:
        chain.step(None, [], [spills[placed]])
        placed += 1
    (first_spill,) = chain.step(None, [], [], [(0, WIN, WIN)], side_low_spill)
    first_spill = shifted(first_spill, "gx", 1)
    for spill in spills[placed:]:
        chain.step(None, [], [spill])
    chain.step(None, [], [(0, first_spill), (0, side_own_spill)])
    return chain.out.reshape(object_field.shape)


def solution(mesh):
    in_specs = (
        P(None, None, "gx", "gy"),
        P(),
        P(),
        P(("gx", "gy"), None, None),
        P(("gx", "gy")),
        P(("gx", "gy"), None),
    )
    out_specs = P(None, None, "gx", "gy")
    return jax.shard_map(body, mesh=mesh, in_specs=in_specs, out_specs=out_specs, check_vma=False)
```

```python
import functools

import jax
import jax.numpy as jnp
from jax import lax
from jax.experimental import pallas as pl
from jax.experimental.pallas import tpu as pltpu
from jax.sharding import PartitionSpec as P

LANE = 128
WIN = 256
COLS = 2048
SLICES = 2
PLANES = 2 * SLICES
SLOTS = 16
TILES = (COLS + WIN) // LANE
RING = 8
KEPT = RING + WIN // LANE
IN_CUTS = (0, 512, 768, 1152, 1536, 1920, 2048)
GROUP_CUTS = (0, 256, 512, 896, 1280, 1664, 2048)
LAG = 3
BATCHES = (2, 1)
VMEM_BYTES = 8 * 1024 * 1024
F32, BF16 = jnp.float32, jnp.bfloat16

SMEM_SPEC = pl.BlockSpec(memory_space=pltpu.SMEM)
VMEM_SPEC = pl.BlockSpec(memory_space=pltpu.VMEM)
HBM_SPEC = pl.BlockSpec(memory_space=pl.ANY)


def shifted(x, axis, by):
    size = lax.axis_size(axis)
    pairs = [(i, i + by) for i in range(size) if 0 <= i + by < size]
    return lax.ppermute(x, axis, pairs)


def params():
    return pltpu.CompilerParams(vmem_limit_bytes=VMEM_BYTES)


def rows_loop(count, step, body):
    def one(index, _):
        body(pl.ds(pl.multiple_of(index * step, step), step), index * step)
        return 0

    lax.fori_loop(0, count // step, one, 0)


def widen(buffer, field, first, width, row_base):
    def some(rows, at):
        target = pl.ds(pl.multiple_of(row_base + at, 64), 64)
        for plane in range(PLANES):
            for tile in range(width // LANE):
                at_tile = first // LANE + tile
                place = at_tile % RING if first < COLS else at_tile - COLS // LANE + RING
                field[plane, place, target, :] = buffer[
                    plane, rows, tile * LANE : (tile + 1) * LANE].astype(F32)

    rows_loop(buffer.shape[1], 64, some)


def start_kernel(field, total):
    def clear(tile, _):
        total[:, tile] = jnp.zeros((PLANES, 2 * WIN, LANE), F32)
        return 0

    lax.fori_loop(0, TILES, clear, 0)
    field[0, 0, 0:8, :] = jnp.zeros((8, LANE), F32)


def process(chosen, offsets, field, total, intensity, left_form, right_form, probe_ref, chi,
            half, waves, kept):
    lane = lax.broadcasted_iota(jnp.int32, (WIN, LANE), 1)
    places = []
    for index in chosen:
        row, col = offsets[2 * index], offsets[2 * index + 1]
        tile = col // LANE
        shift = col - tile * LANE
        places.append((pl.ds(row, WIN), tile, shift))
    count = len(chosen)
    probe = (probe_ref[0], probe_ref[1])
    spread = WIN // LANE
    span = (slice(0, WIN), slice(WIN, 2 * WIN))

    def dot(a, b):
        return jnp.dot(a, b, preferred_element_type=F32)

    def window(k, plane):
        rows, tile, shift = places[k]
        back = lax.rem(LANE - shift, LANE)
        turned = []
        for j in range(spread + 1):
            at = tile + j
            place = jnp.where(at < COLS // LANE, lax.rem(at, RING), at - COLS // LANE + RING)
            turned.append(pltpu.roll(field[plane, place, rows, :], back, 1))
        return jnp.concatenate(
            [jnp.where(lane < LANE - shift, turned[j], turned[j + 1]) for j in range(spread)], 1)

    def deposit(k, plane, value):
        rows, tile, shift = places[k]
        turned = [pltpu.roll(value[:, j * LANE : (j + 1) * LANE], shift, 1) for j in range(spread)]
        inside = lane >= shift
        for j in range(spread + 1):
            if j == 0:
                part = jnp.where(inside, turned[0], 0.0)
            elif j == spread:
                part = jnp.where(inside, 0.0, turned[spread - 1])
            else:
                part = jnp.where(inside, turned[j], turned[j - 1])
            total[plane, tile + j, rows, :] += part

    def stack(k, real, imag):
        chi[k, span[0], :] = real.astype(BF16)
        chi[k, span[1], :] = imag.astype(BF16)

    def through(k, first, second):
        middle = dot(first[...], chi[k]).astype(BF16)
        for part in range(2):
            half[k, :, span[part]] = middle[span[part]]
        result = dot(half[k], second[...])
        return result[:, span[0]], result[:, span[1]]

    for level in range(SLICES):
        for k in range(count):
            obj_real, obj_imag = window(k, 2 * level), window(k, 2 * level + 1)
            if level:
                kept[k, level - 1, 0] = obj_real.astype(BF16)
                kept[k, level - 1, 1] = obj_imag.astype(BF16)
            real, imag = (waves[k, level - 1, 0], waves[k, level - 1, 1]) if level else probe
            stack(k, real * obj_real - imag * obj_imag, real * obj_imag + imag * obj_real)
        for k in range(count):
            real, imag = through(k, left_form, right_form)
            if level < SLICES - 1:
                waves[k, level, 0] = real
                waves[k, level, 1] = imag
            else:
                misfit = real * real + imag * imag - intensity[chosen[k]].astype(F32)
                stack(k, misfit * real, misfit * imag)
    for level in reversed(range(SLICES)):
        for k in range(count):
            lit_real, lit_imag = through(k, right_form, left_form)
            if level:
                obj_real = kept[k, level - 1, 0].astype(F32)
                obj_imag = kept[k, level - 1, 1].astype(F32)
                stack(k, obj_real * lit_real + obj_imag * lit_imag,
                      obj_real * lit_imag - obj_imag * lit_real)
            real, imag = (waves[k, level - 1, 0], waves[k, level - 1, 1]) if level else probe
            deposit(k, 2 * level, real * lit_real + imag * lit_imag)
            deposit(k, 2 * level + 1, real * lit_imag - imag * lit_real)


def step_kernel(plan, *refs):
    refs = list(refs)

    def take(count):
        taken = refs[:count]
        del refs[:count]
        return taken

    if plan["number"] is not None:
        counts, offsets = take(2)
        intensity, left_form, right_form, probe = take(4)
    fresh = take(len(plan["fresh"]))
    landed = take(len(plan["landed"]))
    side = take(1) if plan["mix"] else None
    take(2)
    if plan["has_out"]:
        take(1)
    field, total = take(2)
    if plan["landed"]:
        (out,) = take(1)
    gives = take(len(plan["gives"]))
    placed, out_sems = take(2)
    if plan["number"] is not None:
        chi, half, waves, kept, members = take(5)

    for at, (first, width, row_base) in enumerate(plan["fresh"]):
        widen(fresh[at], field, first, width, row_base)

    if plan["number"] is not None:
        static = (offsets, field, total, intensity, left_form, right_form, probe, chi, half,
                  waves, kept)
        start, stop = GROUP_CUTS[plan["number"]], GROUP_CUTS[plan["number"] + 1]

        def collect(index, found):
            col = offsets[2 * index + 1]
            inside = (index < counts[0]) & (col >= start) & (col < stop)

            @pl.when(inside)
            def _():
                members[found] = index

            return found + inside.astype(jnp.int32)

        found = lax.fori_loop(0, SLOTS, collect, 0)
        at = 0
        for size in BATCHES:

            def batch(index, first, size=size):
                process([members[first + k] for k in range(size)], *static)
                return first + size

            at = lax.fori_loop(0, (found - at) // size, batch, at)

    sends = []
    for at, (first, width, row_base) in enumerate(plan["gives"]):
        add_side = plan["mix"]

        def narrow(rows, offset):
            source = pl.ds(pl.multiple_of(row_base + offset, 64), 64)
            for plane in range(PLANES):
                for tile in range(width // LANE):
                    cols = slice(tile * LANE, (tile + 1) * LANE)
                    value = total[plane, first // LANE + tile, source, :]
                    if add_side:
                        value = value + side[0][plane, rows, cols].astype(F32)
                    gives[at][plane, rows, cols] = value.astype(BF16)

        rows_loop(WIN, 64, narrow)

    groups = {}
    for at, (first, width) in enumerate(plan["landed"]):
        groups.setdefault((first, width), []).append(at)
    done = 0
    for (first, width), members_at in groups.items():

        def add(rows, offset):
            for plane in range(PLANES):
                for tile in range(width // LANE):
                    cols = slice(tile * LANE, (tile + 1) * LANE)
                    value = total[plane, first // LANE + tile, rows, :]
                    for at in members_at:
                        value = value + landed[at][plane, rows, cols].astype(F32)
                    placed[done, plane, rows, cols] = value

        rows_loop(WIN, 64, add)
        sends.append(pltpu.make_async_copy(placed.at[done, :, :, pl.ds(0, width)],
                                           out.at[:, :, pl.ds(first, width)],
                                           out_sems.at[len(sends)]))
        sends[-1].start()
        done += 1
    for copy in sends:
        copy.wait()


class Chain:
    def __init__(self, probe, propagator, measured, counts, offsets):
        real, imag = propagator[0], propagator[1]
        left_form = jnp.concatenate(
            [jnp.concatenate([real, -imag], 1), jnp.concatenate([imag, real], 1)], 0)
        self.counts, self.offsets, self.out = counts, offsets.reshape(-1), None
        self.constants = (measured, left_form, left_form.T, probe)
        self.field, self.total = pl.pallas_call(
            start_kernel,
            out_shape=[pltpu.VMEM((PLANES, KEPT, 2 * WIN, LANE), F32),
                       pltpu.VMEM((PLANES, TILES, 2 * WIN, LANE), F32)],
            out_specs=[VMEM_SPEC] * 2,
            compiler_params=params(),
            cost_estimate=pl.CostEstimate(flops=2**20, bytes_accessed=2**20, transcendentals=0),
            name="begin",
        )()

    def step(self, number=None, fresh=(), landed=(), gives=(), mix=None):
        plan = {
            "number": number,
            "fresh": [(first, x.shape[2], row) for first, row, x in fresh],
            "landed": [(first, x.shape[2]) for first, x in landed],
            "gives": list(gives),
            "mix": mix is not None,
            "has_out": self.out is not None and len(landed) > 0,
        }
        args, specs = [], []
        if number is not None:
            args += [self.counts, self.offsets, *self.constants]
            specs += [SMEM_SPEC] * 2 + [VMEM_SPEC] * 4
        args += [x for _, _, x in fresh] + [x for _, x in landed]
        specs += [VMEM_SPEC] * (len(fresh) + len(landed))
        if mix is not None:
            args.append(mix)
            specs.append(VMEM_SPEC)
        alias = {len(args): 0, len(args) + 1: 1}
        args += [self.field, self.total]
        specs += [VMEM_SPEC] * 2
        outs = [pltpu.VMEM(self.field.shape, F32), pltpu.VMEM(self.total.shape, F32)]
        out_specs = [VMEM_SPEC] * 2
        if landed:
            if self.out is not None:
                alias[len(args)] = 2
                args.append(self.out)
                specs.append(HBM_SPEC)
            outs.append(jax.ShapeDtypeStruct((PLANES, WIN, COLS), F32))
            out_specs.append(HBM_SPEC)
        outs += [jax.ShapeDtypeStruct((PLANES, WIN, width), BF16) for _, width, _ in gives]
        out_specs += [VMEM_SPEC] * len(gives)

        def widest(widths):
            return max([LANE, *widths])

        placed = len({first for first, _ in landed})
        scratch = [
            pltpu.VMEM((max(1, placed), PLANES, WIN, widest(x.shape[2] for _, x in landed)), F32),
            pltpu.SemaphoreType.DMA((max(1, placed),)),
        ]
        if number is not None:
            most = BATCHES[0]
            scratch += [pltpu.VMEM((most, 2 * WIN, WIN), BF16),
                        pltpu.VMEM((most, WIN, 2 * WIN), BF16),
                        pltpu.VMEM((most, SLICES - 1, 2, WIN, WIN), F32),
                        pltpu.VMEM((most, SLICES - 1, 2, WIN, WIN), BF16),
                        pltpu.SMEM((SLOTS,), jnp.int32)]
        result = pl.pallas_call(
            functools.partial(step_kernel, plan),
            out_shape=outs,
            in_specs=specs,
            out_specs=out_specs,
            scratch_shapes=scratch,
            input_output_aliases=alias,
            compiler_params=params(),
            cost_estimate=pl.CostEstimate(flops=2**20, bytes_accessed=2**20, transcendentals=0),
            name="place" if number is None else "group",
        )(*args)
        self.field, self.total = result[:2]
        rest = list(result[2:])
        if landed:
            self.out = rest.pop(0)
        return rest


def body(object_field, probe_field, propagator, measured, counts, offsets):
    own = object_field.reshape(PLANES, WIN, COLS)
    lows = []
    for first, end in zip(IN_CUTS[:-1], IN_CUTS[1:]):
        upper = own[:, :, first:end]
        lows.append((first, upper, shifted(upper, "gx", -1)))
    side_own = shifted(own[:, :, :WIN], "gy", -1)
    side_low = shifted(lows[0][2][:, :, :WIN], "gy", -1)
    chain = Chain(probe_field, propagator, measured, counts, offsets)

    groups = list(zip(GROUP_CUTS[:-1], GROUP_CUTS[1:]))
    spills, placed = [], 0
    taken = 0
    for number, (start, stop) in enumerate(groups):
        final = number == len(groups) - 1
        fresh = []
        while taken < len(lows) and lows[taken][0] < stop + WIN:
            fresh.append((lows[taken][0], 0, lows[taken][1]))
            fresh.append((lows[taken][0], WIN, lows[taken][2]))
            taken += 1
        if number == 1:
            fresh.append((COLS, 0, side_own))
        if number == 2:
            fresh.append((COLS, WIN, side_low))
        landed = []
        if len(spills) - placed >= LAG:
            landed = [spills[placed]]
            placed += 1
        first = max(start, WIN)
        gives = [(first, stop - first, WIN)] if stop > first else []
        if final:
            gives = [(COLS, WIN, WIN)] + gives + [(COLS, WIN, 0)]
        given = chain.step(number, fresh, landed, gives)
        if final:
            side_low_spill = shifted(given[0], "gy", 1)
            spills.append((first, shifted(given[1], "gx", 1)))
            side_own_spill = shifted(given[2], "gy", 1)
        elif gives:
            spills.append((first, shifted(given[0], "gx", 1)))
    while placed < len(spills) - 1:
        chain.step(None, [], [spills[placed]])
        placed += 1
    (first_spill,) = chain.step(None, [], [], [(0, WIN, WIN)], side_low_spill)
    first_spill = shifted(first_spill, "gx", 1)
    for spill in spills[placed:]:
        chain.step(None, [], [spill])
    chain.step(None, [], [(0, first_spill), (0, side_own_spill)])
    return chain.out.reshape(object_field.shape)


def solution(mesh):
    in_specs = (
        P(None, None, "gx", "gy"),
        P(),
        P(),
        P(("gx", "gy"), None, None),
        P(("gx", "gy")),
        P(("gx", "gy"), None),
    )
    out_specs = P(None, None, "gx", "gy")
    return jax.shard_map(body, mesh=mesh, in_specs=in_specs, out_specs=out_specs, check_vma=False)
```
